1024 devices in a mesh: fsdp: 32 (over z, x_lo), dp: 32 (over y, x_hi, core).
Axes of the slice: x: 8 (x_hi: 2, x_lo: 4; x = x_hi * 4 + x_lo), y: 8, z: 8, core: 2. Of those that a mesh axis runs over, the one named last changes fastest.
Arguments:
- tokens: bfloat16 [32, 6144, 4096], P('dp', 'fsdp'), may hold values from -9 to 9
- segment_ids: int32 [32, 6144], P('dp'), may hold values from 0 to 95, never falling along the last dimension, each value on 1 to 192 neighbouring positions
- w_query: bfloat16 [4096, 128], P('fsdp'), may hold values from -0.2 to 0.2
- w_key: bfloat16 [4096, 128], P('fsdp'), may hold values from -0.2 to 0.2
- w_value: bfloat16 [4096, 128], P('fsdp'), may hold values from -0.09375 to 0.09375
- grad_out: bfloat16 [32, 6144, 128], P('dp', 'fsdp'), may hold values from -6 to 6
Outputs:
- attn: bfloat16 [32, 6144, 128], P('dp', 'fsdp')
- grad_tokens: bfloat16 [32, 6144, 4096], P('dp', 'fsdp')
- grad_query: float32 [4096, 128], P(('fsdp', 'dp'))
- grad_key: float32 [4096, 128], P(('fsdp', 'dp'))
- grad_value: float32 [4096, 128], P(('fsdp', 'dp'))
The draws below stay inside these ranges and needn't reach their ends.
Inputs may be any that keep to these rules, and one draw needn't show every extreme that they name: `segment_ids`: ids never fall along a sequence; every document has 1 to 192 tokens and some document has exactly 192.
All inputs are finite; a program needn't handle non-finite values.
Results may differ from the reference program's by a relative error of at most 0.03.
Values may be sent and summed in bfloat16 or wider, within the bound.
No kernel may reach another device: no remote copies, remote signals or barrier semaphores. Data moves between devices by JAX's collectives and lax.ppermute only.
A program may use at most 32 MiB of HBM per device.

```python
import math
import jax
import jax.numpy as jnp
import numpy as np
from jax import lax

D = 4096
HD = 128
TOK_DEV = 192
SEQ = 6144
GROUPS = 32
DOCS = 96


def draw_tokens(key, part):
    key = jax.random.fold_in(key, 5)
    first = jax.random.fold_in(key, 0)
    values = jnp.clip(jax.random.normal(first, (GROUPS, SEQ, D), jnp.float32), -6.0, 6.0)
    return values.astype(jnp.bfloat16)


def draw_w_query(key, part):
    key = jax.random.fold_in(key, 11)
    values = jax.random.normal(key, (D, HD), jnp.float32) / math.sqrt(D)
    return jnp.clip(values, -0.2, 0.2).astype(jnp.bfloat16)


def draw_w_key(key, part):
    key = jax.random.fold_in(key, 17)
    own_part = jax.random.normal(key, (D, HD), jnp.float32) / math.sqrt(D)
    values = own_part
    return jnp.clip(values, -0.2, 0.2).astype(jnp.bfloat16)


def levels(key, dims, cuts, low, largest):
    def one(position, blocks):
        heights = jax.random.uniform(jax.random.fold_in(jax.random.fold_in(key, 6), position), (blocks,), jnp.float32, low / len(cuts), largest / len(cuts))
        return jnp.repeat(jnp.exp(heights), dims[position] // blocks).reshape((-1,) + (1,) * (len(dims) - position - 1))

    loudness = one(*cuts[0])
    for cut in cuts[1:]:
        loudness = loudness * one(*cut)
    return loudness


def split_up(number_of, total, most, slope):
    loads = [(1 << 20) // math.isqrt(grade ** slope) + 1 for grade in range(2, number_of + 1)]
    surplus, counts = total - most - (number_of - 1), [1] * (number_of - 1)
    while surplus > 0:
        free = [i for i in range(number_of - 1) if counts[i] < most]
        mass, left = sum([loads[i] for i in free]), surplus
        for i in free:
            more = min(most - counts[i], max(1, left * loads[i] // mass), surplus)
            counts[i] = counts[i] + more
            surplus = surplus - more
    return np.array([most] + counts)


def uneven_parts(own_key, amount, total, limit, lean):
    if amount == 2:
        one = jax.random.randint(own_key, (), max(1, total - limit), min(limit, total - 1) + 1)
        return jnp.stack([one, total - one])
    lengths = jnp.asarray(split_up(amount, total, limit, lean), jnp.int32)
    twos = (amount - 1) // 2
    source_of, taker = lengths[1:1 + 2 * twos:2], lengths[2:2 + 2 * twos:2]
    slack = jnp.minimum(source_of - 1, limit - taker)
    moved = jax.random.randint(jax.random.fold_in(own_key, 1), (twos,), 0, 1 << 20) % (slack + 1)
    lengths = lengths.at[1:1 + 2 * twos:2].set(source_of - moved).at[2:2 + 2 * twos:2].set(taker + moved)
    return lengths[jax.random.permutation(jax.random.fold_in(own_key, 2), amount)]


def scatter_about(stream_key, shape, spread, bound, cuts=(), kind=jnp.bfloat16):
    entries = spread * jax.random.normal(stream_key, shape, jnp.float32)
    if cuts:
        entries = entries * levels(stream_key, shape, cuts, -0.22, 0.18)
    return jnp.clip(entries, -bound, bound).astype(kind)


def setup_inputs(seed: int = 0) -> dict:
    keys = jax.random.split(jax.random.key(seed), 7)
    return {
        "tokens": draw_tokens(jax.random.fold_in(keys[6], 71), 0),
        "segment_ids": jax.vmap(lambda own: jnp.searchsorted(jnp.cumsum(uneven_parts(own, DOCS, SEQ, TOK_DEV, 0)), jnp.arange(SEQ), side="right"))(jax.random.split(keys[1], GROUPS)).reshape((GROUPS, SEQ)).astype(jnp.int32),
        "w_query": draw_w_query(jax.random.fold_in(keys[6], 71), 0),
        "w_key": draw_w_key(jax.random.fold_in(keys[6], 71), 0),
        "w_value": scatter_about(keys[4], (D, HD), D ** -0.5, 0.09375, ((0, 32),)),
        "grad_out": scatter_about(keys[5], (GROUPS, SEQ, HD), 1.0, 6.0, ((0, 32), (1, 32))),
    }


def with_prior(blocks):
    earlier = jnp.concatenate([jnp.zeros_like(blocks[:1]), blocks[:-1]], axis=0)
    return jnp.concatenate([earlier, blocks], axis=1)

def group_pass(weights, tok_rows, id_line, upstream):
    block_count = SEQ // TOK_DEV
    projected = jnp.dot(tok_rows, weights, preferred_element_type=jnp.float32).astype(jnp.bfloat16)
    query_rows = projected[:, :HD].reshape(block_count, TOK_DEV, HD)
    keys_own = projected[:, HD:2 * HD].reshape(block_count, TOK_DEV, HD)
    values_own = projected[:, 2 * HD:].reshape(block_count, TOK_DEV, HD)
    block_ids = id_line.reshape(block_count, TOK_DEV)
    positions = jnp.arange(SEQ, dtype=jnp.int32).reshape(block_count, TOK_DEV)
    packed_key_rows = with_prior(keys_own)
    packed_value_rows = with_prior(values_own)
    key_ids = with_prior(block_ids)
    key_pos = jnp.concatenate([positions - TOK_DEV, positions], axis=1)
    allowed = (key_pos[:, None, :] <= positions[:, :, None]) & (key_pos[:, None, :] >= 0) & (key_ids[:, None, :] == block_ids[:, :, None])
    softmax_scale = 1.0 / math.sqrt(HD)
    logit_scores = jnp.einsum('dns,dws->dnw', query_rows.astype(jnp.float32), packed_key_rows.astype(jnp.float32)) * softmax_scale
    logit_scores = jnp.where(allowed, logit_scores, -1e+30)
    peak = lax.optimization_barrier(jnp.max(logit_scores, axis=-1, keepdims=True))
    weights_exp = jnp.where(allowed, jnp.exp(logit_scores - peak), 0.0)
    prob = weights_exp / lax.optimization_barrier(jnp.sum(weights_exp, axis=-1, keepdims=True))
    probability_batch = prob.astype(jnp.bfloat16)
    attn = jnp.einsum('jpi,jia->jpa', probability_batch.astype(jnp.float32), packed_value_rows.astype(jnp.float32)).astype(jnp.bfloat16)
    incoming_gradient_batch = upstream.reshape(block_count, TOK_DEV, HD)
    probability_gradient = jnp.einsum('dns,dws->dnw', incoming_gradient_batch.astype(jnp.float32), packed_value_rows.astype(jnp.float32))
    delta = lax.optimization_barrier(jnp.sum(prob * probability_gradient, axis=-1, keepdims=True))
    score_gradient = (prob * (probability_gradient - delta) * softmax_scale).astype(jnp.bfloat16)
    query_gradient = jnp.einsum('jpi,jia->jpa', score_gradient.astype(jnp.float32), packed_key_rows.astype(jnp.float32)).astype(jnp.bfloat16)
    key_gradient_parts = jnp.einsum('foy,foi->fyi', score_gradient.astype(jnp.float32), query_rows.astype(jnp.float32))
    value_gradient_parts = jnp.einsum('foy,foi->fyi', probability_batch.astype(jnp.float32), incoming_gradient_batch.astype(jnp.float32))

    def settle(terms):
        later = jnp.concatenate([terms[1:, :TOK_DEV], jnp.zeros_like(terms[:1, :TOK_DEV])], axis=0)
        return (terms[:, TOK_DEV:] + later).astype(jnp.bfloat16)
    grad_k = settle(key_gradient_parts)
    grad_v = settle(value_gradient_parts)
    grad_proj = jnp.concatenate([query_gradient, grad_k, grad_v], axis=-1)
    grad_flat = grad_proj.reshape(SEQ, 3 * HD)
    grad_rows_out = lax.dot_general(grad_flat, weights, (((1,), (1,)), ((), ())), preferred_element_type=jnp.float32).astype(jnp.bfloat16)
    partial_terms = jnp.einsum('btd,btc->bdc', tok_rows.reshape(block_count, TOK_DEV, D).astype(jnp.float32), grad_proj.astype(jnp.float32))
    partial_terms = lax.optimization_barrier(partial_terms.astype(jnp.bfloat16))
    weight_sum = lax.optimization_barrier(jnp.sum(partial_terms.astype(jnp.float32), axis=0))
    return (attn.reshape(SEQ, HD), grad_rows_out, weight_sum)

def reference(tokens, segment_ids, w_query, w_key, w_value, grad_out):
    weights = jnp.concatenate([w_query, w_key, w_value], axis=1)

    def step(running, inputs):
        attn, grad_rows_out, weight_sum = group_pass(weights, inputs[0], inputs[1], inputs[2])
        return (running + weight_sum, (attn, grad_rows_out))
    running, stacked = lax.scan(step, jnp.zeros((D, 3 * HD), jnp.float32), (tokens, segment_ids, grad_out))
    grads = running * (1.0 / math.sqrt(GROUPS * SEQ))
    return (stacked[0], stacked[1], grads[:, :HD], grads[:, HD:2 * HD], grads[:, 2 * HD:])
```

```python
import functools
import math

import jax
import jax.numpy as jnp
from jax import lax
from jax.experimental import pallas as pl
from jax.experimental.pallas import tpu as pltpu
from jax.sharding import Mesh
from jax.sharding import PartitionSpec as P

FSDP = ("zh", "zl", "xlh", "xll")
DP = ("yh", "yl", "xh", "c")
SIZES = (4, 2, 2, 2, 4, 2, 2, 2)
CUBE = ("zl", "xll", "yl")
SWAP = [(0, 1), (1, 0)]
VMEM = 48 * 1024 * 1024


def fsdp_index(zh, zl, xlh, xll):
    return ((zh * 2 + zl) * 2 + xlh) * 2 + xll


def shifted(block, distance):
    route = [(i - distance, i) for i in range(32) if 0 <= i - distance < 32]
    return lax.ppermute(block, FSDP, route)


def project_kernel(core_ref, tok_ref, mine_ref, other_ref, weight_ref, qkv_ref):
    core = core_ref[0]
    for zl in range(2):
        for xll in range(2):
            for yl in range(2):
                for zh in range(4):
                    for xlh in range(2):
                        row = fsdp_index(zh, zl, xlh, xll) * 128 + yl * 32
                        at = (zl * 2 + xll) * 2 + yl, zh * 2 + xlh
                        here = pl.multiple_of(row + core * 64, 32)
                        there = pl.multiple_of(row + (1 - core) * 64, 32)
                        weight_ref[pl.ds(here, 32), :] = mine_ref[at]
                        weight_ref[pl.ds(there, 32), :] = other_ref[at]
    qkv_ref[...] = jnp.dot(
        tok_ref[...], weight_ref[...], preferred_element_type=jnp.float32
    ).astype(jnp.bfloat16)


def term_kernel(core_ref, tok_ref, grad_ref, mine_ref, other_ref):
    first = core_ref[0] == 0
    grad = grad_ref[...]
    columns = grad.shape[1]
    low = lax.broadcasted_iota(jnp.int32, (8, 8, columns), 1) < 4
    for zh in range(4):
        for zl in range(2):
            for xlh in range(2):
                for xll in range(2):
                    f = fsdp_index(zh, zl, xlh, xll)
                    term = lax.dot_general(
                        tok_ref[:, f * 128 : (f + 1) * 128],
                        grad,
                        (((0,), (0,)), ((), ())),
                        preferred_element_type=jnp.float32,
                    )
                    by_hi = term.reshape(8, 2, 8, columns)
                    even, odd = by_hi[:, 0], by_hi[:, 1]
                    zero = jnp.where(low, even, pltpu.roll(odd, 4, 1))
                    one = jnp.where(low, pltpu.roll(even, 4, 1), odd)
                    mine = jnp.where(first, zero, one).reshape(4, 2, 8, columns)
                    other = jnp.where(first, one, zero).reshape(4, 2, 8, columns)
                    for yl in range(2):
                        at = (zl * 2 + xll) * 2 + yl, zh * 2 + xlh
                        mine_ref[at] = mine[:, yl].reshape(32, columns).astype(jnp.bfloat16)
                        other_ref[at] = other[:, yl].reshape(32, columns).astype(jnp.bfloat16)


def whole(memory=pltpu.VMEM):
    return pl.BlockSpec(memory_space=memory)


def call(kernel, outs, flops, moved, *args):
    return pl.pallas_call(
        kernel,
        out_shape=[jax.ShapeDtypeStruct(shape, jnp.bfloat16) for shape in outs],
        in_specs=[whole(pltpu.SMEM)] + [whole() for _ in args[1:]],
        out_specs=[whole() for _ in outs],
        compiler_params=pltpu.CompilerParams(vmem_limit_bytes=VMEM),
        cost_estimate=pl.CostEstimate(flops=flops, bytes_accessed=moved, transcendentals=0),
    )(*args)


def local(tokens, segment_ids, w_query, w_key, w_value, grad_out):
    tok_rows = tokens[0]
    tok_count, depth = tok_rows.shape
    heads = w_query.shape[1]
    core = lax.axis_index("c")
    core_arg = core.reshape(1).astype(jnp.int32)
    flops, moved = 2 * tok_count * depth * 3 * heads, 3 * 2 * tok_count * depth

    local_weight = jnp.concatenate([w_query, w_key, w_value], axis=1)
    start = core * 64 + lax.axis_index("yl") * 32
    quarter = lax.dynamic_slice_in_dim(local_weight, start, 32, axis=0)
    far = lax.all_to_all(jnp.broadcast_to(quarter, (8,) + quarter.shape), ("zh", "xlh"), 0, 0)
    half = lax.all_to_all(jnp.broadcast_to(far, (8,) + far.shape), CUBE, 0, 0)
    other_half = lax.ppermute(half, "c", SWAP)
    full_weight, qkv_rounded = call(
        project_kernel,
        [(depth, 3 * heads), (tok_count, 3 * heads)],
        flops,
        moved,
        core_arg,
        tok_rows,
        half,
        other_half,
    )

    query_rows = qkv_rounded[:, :heads]
    own_keys = qkv_rounded[:, heads : 2 * heads]
    own_values = qkv_rounded[:, 2 * heads :]
    earlier = shifted(qkv_rounded[:, heads:], 1)
    packed_key_rows = jnp.concatenate([earlier[:, :heads], own_keys], axis=0)
    packed_value_rows = jnp.concatenate([earlier[:, heads:], own_values], axis=0)
    device = lax.axis_index(FSDP)
    first_row = device * tok_count
    id_line = segment_ids[0]
    own_ids = lax.dynamic_slice_in_dim(id_line, first_row, tok_count)
    prior_ids = lax.dynamic_slice_in_dim(id_line, jnp.maximum(first_row - tok_count, 0), tok_count)
    key_ids = jnp.concatenate([prior_ids, own_ids])
    query_pos = first_row + jnp.arange(tok_count, dtype=jnp.int32)
    key_pos = first_row - tok_count + jnp.arange(2 * tok_count, dtype=jnp.int32)
    allowed = (
        (key_pos[None, :] <= query_pos[:, None])
        & (key_pos[None, :] >= 0)
        & (key_ids[None, :] == own_ids[:, None])
    )
    softmax_scale = 1.0 / math.sqrt(heads)
    logit_scores = (
        lax.dot_general(
            query_rows,
            packed_key_rows,
            (((1,), (1,)), ((), ())),
            preferred_element_type=jnp.float32,
        )
        * softmax_scale
    )
    logit_scores = jnp.where(allowed, logit_scores, -1e30)
    peak = jnp.max(logit_scores, axis=-1, keepdims=True)
    weights_exp = jnp.where(allowed, jnp.exp(logit_scores - peak), 0.0)
    prob = weights_exp / jnp.sum(weights_exp, axis=-1, keepdims=True)
    probability_batch = prob.astype(jnp.bfloat16)
    attn = jnp.dot(probability_batch, packed_value_rows, preferred_element_type=jnp.float32).astype(
        jnp.bfloat16
    )
    upstream = grad_out[0]
    probability_gradient = lax.dot_general(
        upstream, packed_value_rows, (((1,), (1,)), ((), ())), preferred_element_type=jnp.float32
    )
    delta = jnp.sum(prob * probability_gradient, axis=-1, keepdims=True)
    score_gradient = (prob * (probability_gradient - delta) * softmax_scale).astype(jnp.bfloat16)
    query_gradient = jnp.dot(
        score_gradient, packed_key_rows, preferred_element_type=jnp.float32
    ).astype(jnp.bfloat16)
    key_gradient_parts = lax.dot_general(
        score_gradient, query_rows, (((0,), (0,)), ((), ())), preferred_element_type=jnp.float32
    )
    value_gradient_parts = lax.dot_general(
        probability_batch, upstream, (((0,), (0,)), ((), ())), preferred_element_type=jnp.float32
    )
    returned = shifted(
        jnp.stack([key_gradient_parts[:tok_count], value_gradient_parts[:tok_count]]), -1
    )
    grad_k = (key_gradient_parts[tok_count:] + returned[0]).astype(jnp.bfloat16)
    grad_v = (value_gradient_parts[tok_count:] + returned[1]).astype(jnp.bfloat16)
    grad_proj = jnp.concatenate([query_gradient, grad_k, grad_v], axis=1)

    parts = (8, 8, 32, 3 * heads)
    mine, other = call(
        term_kernel, [parts, parts], flops, moved, core_arg, tok_rows, grad_proj
    )
    swapped = lax.ppermute(other, "c", SWAP)
    grad_input = lax.dot_general(
        grad_proj, full_weight, (((1,), (1,)), ((), ())), preferred_element_type=jnp.float32
    ).astype(jnp.bfloat16)
    chip = (mine.astype(jnp.float32) + swapped.astype(jnp.float32)).astype(jnp.bfloat16)
    cube = jnp.sum(lax.all_to_all(chip, CUBE, 0, 0).astype(jnp.float32), axis=0)
    rows = cube.astype(jnp.bfloat16).reshape(64, 4, 3 * heads)
    rows = lax.all_to_all(rows, ("zh", "xlh", "yh", "xh"), 0, 0)
    count = math.prod(lax.axis_size(name) for name in FSDP + DP) * tok_count
    grads = jnp.sum(rows.astype(jnp.float32), axis=0) * (1.0 / math.sqrt(count))
    return (
        attn[None],
        grad_input[None],
        grads[:, :heads],
        grads[:, heads : 2 * heads],
        grads[:, 2 * heads :],
    )


def solution(mesh):
    fine = Mesh(mesh.devices.reshape(SIZES), FSDP + DP)
    rows = P(DP, FSDP, None)
    weight = P(FSDP, None)
    gradient = P(FSDP + DP, None)
    return jax.shard_map(
        local,
        mesh=fine,
        in_specs=(rows, P(DP, None), weight, weight, weight, rows),
        out_specs=(rows, rows, gradient, gradient, gradient),
        check_vma=False,
    )
```

```python
import math

import jax
import jax.numpy as jnp
from jax import lax
from jax.experimental import pallas as pl
from jax.experimental.pallas import tpu as pltpu
from jax.sharding import Mesh
from jax.sharding import PartitionSpec as P

FSDP = ("zh", "zl", "xlh", "xll")
DP = ("yh", "yl", "xh", "c")
SIZES = (4, 2, 2, 2, 4, 2, 2, 2)
CUBE = ("zl", "xll", "yl")
SWAP = [(0, 1), (1, 0)]
VMEM = 20 * 1024 * 1024


def fsdp_index(zh, zl, xlh, xll):
    return ((zh * 2 + zl) * 2 + xlh) * 2 + xll


def shifted(block, distance):
    route = [(i - distance, i) for i in range(32) if 0 <= i - distance < 32]
    return lax.ppermute(block, FSDP, route)


def project_kernel(core_ref, tok_ref, mine_ref, other_ref, weight_ref, qkv_ref):
    core = core_ref[0]
    for zl in range(2):
        for xll in range(2):
            for yl in range(2):
                for zh in range(4):
                    for xlh in range(2):
                        row = fsdp_index(zh, zl, xlh, xll) * 128 + yl * 32
                        at = (zl * 2 + xll) * 2 + yl, zh * 2 + xlh
                        here = pl.multiple_of(row + core * 64, 32)
                        there = pl.multiple_of(row + (1 - core) * 64, 32)
                        weight_ref[pl.ds(here, 32), :] = mine_ref[at]
                        weight_ref[pl.ds(there, 32), :] = other_ref[at]
    qkv_ref[...] = jnp.dot(
        tok_ref[...], weight_ref[...], preferred_element_type=jnp.float32
    ).astype(jnp.bfloat16)


def attend_kernel(
    qkv_ref, earlier_ref, query_ids_ref, key_ids_ref, upstream_ref, attn_ref, dq_ref, own_ref, back_ref
):
    tok_count, heads = dq_ref.shape
    scale = 1.0 / math.sqrt(heads)
    query = qkv_ref[:, :heads]
    keys = jnp.concatenate([earlier_ref[:, :heads], qkv_ref[:, heads : 2 * heads]], axis=0)
    values = jnp.concatenate([earlier_ref[:, heads:], qkv_ref[:, 2 * heads :]], axis=0)
    upstream = upstream_ref[...]
    across, over = (((1,), (1,)), ((), ())), (((0,), (0,)), ((), ()))

    def dot(a, b, dims):
        return lax.dot_general(a, b, dims, preferred_element_type=jnp.float32)

    rows = lax.broadcasted_iota(jnp.int32, (tok_count, 2 * tok_count), 0)
    columns = lax.broadcasted_iota(jnp.int32, (tok_count, 2 * tok_count), 1)
    allowed = (columns <= rows + tok_count) & (key_ids_ref[...] == query_ids_ref[...])
    scores = jnp.where(allowed, dot(query, keys, across) * scale, -1e30)
    peak = jnp.max(scores, axis=-1, keepdims=True)
    raised = jnp.where(allowed, jnp.exp(scores - peak), 0.0)
    prob = raised / jnp.sum(raised, axis=-1, keepdims=True)
    prob_b = prob.astype(jnp.bfloat16)
    dprob = dot(upstream, values, across)
    delta = jnp.sum(prob * dprob, axis=-1, keepdims=True)
    dscore = (prob * (dprob - delta) * scale).astype(jnp.bfloat16)
    dk = dot(dscore, query, over)
    dv = dot(prob_b, upstream, over)
    back_ref[:, :heads] = dk[:tok_count].astype(jnp.bfloat16)
    back_ref[:, heads:] = dv[:tok_count].astype(jnp.bfloat16)
    own_ref[:, :heads] = dk[tok_count:]
    own_ref[:, heads:] = dv[tok_count:]
    dq_ref[...] = jnp.dot(dscore, keys, preferred_element_type=jnp.float32).astype(jnp.bfloat16)
    attn_ref[...] = jnp.dot(prob_b, values, preferred_element_type=jnp.float32).astype(jnp.bfloat16)


def term_kernel(core_ref, tok_ref, dq_ref, own_ref, back_ref, mine_ref, other_ref, grad_ref):
    first = core_ref[0] == 0
    heads = dq_ref.shape[1]
    grad_ref[:, :heads] = dq_ref[...]
    grad_ref[:, heads:] = (own_ref[...] + back_ref[...].astype(jnp.float32)).astype(jnp.bfloat16)
    grad = grad_ref[...]
    columns = grad.shape[1]
    low = lax.broadcasted_iota(jnp.int32, (8, 8, columns), 1) < 4
    for zh in range(4):
        for zl in range(2):
            for xlh in range(2):
                for xll in range(2):
                    f = fsdp_index(zh, zl, xlh, xll)
                    term = lax.dot_general(
                        tok_ref[:, f * 128 : (f + 1) * 128],
                        grad,
                        (((0,), (0,)), ((), ())),
                        preferred_element_type=jnp.float32,
                    )
                    by_hi = term.reshape(8, 2, 8, columns)
                    even, odd = by_hi[:, 0], by_hi[:, 1]
                    zero = jnp.where(low, even, pltpu.roll(odd, 4, 1))
                    one = jnp.where(low, pltpu.roll(even, 4, 1), odd)
                    mine = jnp.where(first, zero, one).reshape(4, 2, 8, columns)
                    other = jnp.where(first, one, zero).reshape(4, 2, 8, columns)
                    for yl in range(2):
                        at = (zl * 2 + xll) * 2 + yl, zh * 2 + xlh
                        mine_ref[at] = mine[:, yl].reshape(32, columns).astype(jnp.bfloat16)
                        other_ref[at] = other[:, yl].reshape(32, columns).astype(jnp.bfloat16)


def back_kernel(grad_ref, weight_ref, out_ref):
    out_ref[...] = lax.dot_general(
        grad_ref[...], weight_ref[...], (((1,), (1,)), ((), ())), preferred_element_type=jnp.float32
    ).astype(jnp.bfloat16)


def whole(memory=pltpu.VMEM):
    return pl.BlockSpec(memory_space=memory)


def call(kernel, outs, flops, moved, *args):
    scalar = [whole(pltpu.SMEM if arg.ndim == 1 else pltpu.VMEM) for arg in args]
    return pl.pallas_call(
        kernel,
        out_shape=[jax.ShapeDtypeStruct(shape, dtype) for shape, dtype in outs],
        in_specs=scalar,
        out_specs=[whole() for _ in outs],
        compiler_params=pltpu.CompilerParams(vmem_limit_bytes=VMEM),
        cost_estimate=pl.CostEstimate(flops=flops, bytes_accessed=moved, transcendentals=0),
    )(*args)


def input_gradient(grad, weight, flops, moved):
    depth, columns = weight.shape
    wide = 512
    return pl.pallas_call(
        back_kernel,
        grid=(depth // wide,),
        out_shape=jax.ShapeDtypeStruct((grad.shape[0], depth), jnp.bfloat16),
        in_specs=[
            pl.BlockSpec(grad.shape, lambda i: (0, 0)),
            pl.BlockSpec((wide, columns), lambda i: (i, 0)),
        ],
        out_specs=pl.BlockSpec((grad.shape[0], wide), lambda i: (0, i)),
        compiler_params=pltpu.CompilerParams(vmem_limit_bytes=VMEM),
        cost_estimate=pl.CostEstimate(flops=flops, bytes_accessed=moved, transcendentals=0),
    )(grad, weight)


def local(tokens, segment_ids, w_query, w_key, w_value, grad_out):
    tok_rows = tokens[0]
    tok_count, depth = tok_rows.shape
    heads = w_query.shape[1]
    bf16, f32 = jnp.bfloat16, jnp.float32
    core = lax.axis_index("c")
    core_arg = core.reshape(1).astype(jnp.int32)
    flops, moved = 2 * tok_count * depth * 3 * heads, 3 * 2 * tok_count * depth

    local_weight = jnp.concatenate([w_query, w_key, w_value], axis=1)
    start = core * 64 + lax.axis_index("yl") * 32
    quarter = lax.dynamic_slice_in_dim(local_weight, start, 32, axis=0)
    far = lax.all_to_all(jnp.broadcast_to(quarter, (8,) + quarter.shape), ("zh", "xlh"), 0, 0)
    half = lax.all_to_all(jnp.broadcast_to(far, (8,) + far.shape), CUBE, 0, 0)
    other_half = lax.ppermute(half, "c", SWAP)
    full_weight, qkv_rounded = call(
        project_kernel,
        [((depth, 3 * heads), bf16), ((tok_count, 3 * heads), bf16)],
        flops,
        moved,
        core_arg,
        tok_rows,
        half,
        other_half,
    )

    first_row = lax.axis_index(FSDP) * tok_count
    id_line = segment_ids[0]
    own_ids = lax.dynamic_slice_in_dim(id_line, first_row, tok_count)
    prior_ids = lax.dynamic_slice_in_dim(id_line, jnp.maximum(first_row - tok_count, 0), tok_count)
    prior_ids = jnp.where(first_row > 0, prior_ids, -1)
    attn, query_gradient, own_parts, back_parts = call(
        attend_kernel,
        [
            ((tok_count, heads), bf16),
            ((tok_count, heads), bf16),
            ((tok_count, 2 * heads), f32),
            ((tok_count, 2 * heads), bf16),
        ],
        7 * 4 * tok_count * tok_count * heads,
        12 * tok_count * heads,
        qkv_rounded,
        shifted(qkv_rounded[:, heads:], 1),
        own_ids[:, None],
        jnp.concatenate([prior_ids, own_ids])[None, :],
        grad_out[0],
    )
    returned = shifted(back_parts, -1)

    parts = (8, 8, 32, 3 * heads)
    mine, other, grad_proj = call(
        term_kernel,
        [(parts, bf16), (parts, bf16), ((tok_count, 3 * heads), bf16)],
        flops,
        moved,
        core_arg,
        tok_rows,
        query_gradient,
        own_parts,
        returned,
    )
    swapped = lax.ppermute(other, "c", SWAP)
    grad_input = input_gradient(grad_proj, full_weight, flops, moved)
    swapped, grad_input = lax.optimization_barrier((swapped, grad_input))
    chip = (mine.astype(jnp.float32) + swapped.astype(jnp.float32)).astype(jnp.bfloat16)
    cube = jnp.sum(lax.all_to_all(chip, CUBE, 0, 0).astype(jnp.float32), axis=0)
    rows = cube.astype(jnp.bfloat16).reshape(64, 4, 3 * heads)
    rows = lax.all_to_all(rows, ("zh", "xlh", "yh", "xh"), 0, 0)
    count = math.prod(lax.axis_size(name) for name in FSDP + DP) * tok_count
    grads = jnp.sum(rows.astype(jnp.float32), axis=0) * (1.0 / math.sqrt(count))
    return (
        attn[None],
        grad_input[None],
        grads[:, :heads],
        grads[:, heads : 2 * heads],
        grads[:, 2 * heads :],
    )


def solution(mesh):
    fine = Mesh(mesh.devices.reshape(SIZES), FSDP + DP)
    rows = P(DP, FSDP, None)
    weight = P(FSDP, None)
    gradient = P(FSDP + DP, None)
    return jax.shard_map(
        local,
        mesh=fine,
        in_specs=(rows, P(DP, None), weight, weight, weight, rows),
        out_specs=(rows, rows, gradient, gradient, gradient),
        check_vma=False,
    )
```

```python
import math

import jax
import jax.numpy as jnp
from jax import lax
from jax.experimental import pallas as pl
from jax.experimental.pallas import tpu as pltpu
from jax.sharding import Mesh
from jax.sharding import PartitionSpec as P

FSDP = ("zh", "zl", "xlh", "xll")
DP = ("yh", "yl", "xh", "c")
SIZES = (4, 2, 2, 2, 4, 2, 2, 2)
SWAP = [(0, 1), (1, 0)]
VMEM = 20 * 1024 * 1024


def fsdp_index(zh, zl, xlh, xll):
    return ((zh * 2 + zl) * 2 + xlh) * 2 + xll


def cubes():
    def index(z, x, y, core):
        x_hi = x // 4
        fsdp = z * 4 + x % 4
        return ((fsdp * 8 + y) * 2 + x_hi) * 2 + core

    groups = []
    for core in range(2):
        for corner in range(64):
            low = [2 * (corner // 16) + core, 2 * (corner // 4 % 4) + core, 2 * (corner % 4) + core]
            members = []
            for bits in range(8):
                want = (bits // 4, bits // 2 % 2, bits % 2)
                z, x, y = ((a + (a + b) % 2) % 8 for a, b in zip(low, want))
                members.append(index(z, x, y, core))
            groups.append(members)
    return groups


def cube_exchange(block):
    return lax.all_to_all(block, FSDP + DP, 0, 0, axis_index_groups=cubes())


def shifted(block, distance):
    route = [(i - distance, i) for i in range(32) if 0 <= i - distance < 32]
    return lax.ppermute(block, FSDP, route)


def project_kernel(core_ref, tok_ref, mine_ref, other_ref, weight_ref, qkv_ref, *scratch):
    core = core_ref[0]
    total, copies = None, []
    for zh in range(4):
        part_ref, done = scratch[zh], scratch[4].at[zh]
        for zl in range(2):
            for xlh in range(2):
                for xll in range(2):
                    for yl in range(2):
                        row = fsdp_index(0, zl, xlh, xll) * 128 + yl * 32
                        at = (zl * 2 + xll) * 2 + yl, zh * 2 + xlh
                        here = pl.multiple_of(row + core * 64, 32)
                        there = pl.multiple_of(row + (1 - core) * 64, 32)
                        part_ref[pl.ds(here, 32), :] = mine_ref[at]
                        part_ref[pl.ds(there, 32), :] = other_ref[at]
        rows = part_ref.shape[0]
        copy = pltpu.make_async_copy(part_ref, weight_ref.at[pl.ds(zh * rows, rows), :], done)
        copy.start()
        copies.append(copy)
        term = jnp.dot(
            tok_ref[:, zh * rows : (zh + 1) * rows], part_ref[...], preferred_element_type=jnp.float32
        )
        total = term if total is None else total + term
    qkv_ref[...] = total.astype(jnp.bfloat16)
    for copy in copies:
        copy.wait()


def attend_kernel(
    qkv_ref, earlier_ref, query_ids_ref, key_ids_ref, upstream_ref, attn_ref, dq_ref, own_ref, back_ref
):
    tok_count, heads = dq_ref.shape
    scale = 1.0 / math.sqrt(heads)
    query = qkv_ref[:, :heads]
    keys = jnp.concatenate([earlier_ref[:, :heads], qkv_ref[:, heads : 2 * heads]], axis=0)
    values = jnp.concatenate([earlier_ref[:, heads:], qkv_ref[:, 2 * heads :]], axis=0)
    upstream = upstream_ref[...]
    across, over = (((1,), (1,)), ((), ())), (((0,), (0,)), ((), ()))

    def dot(a, b, dims):
        return lax.dot_general(a, b, dims, preferred_element_type=jnp.float32)

    rows = lax.broadcasted_iota(jnp.int32, (tok_count, 2 * tok_count), 0)
    columns = lax.broadcasted_iota(jnp.int32, (tok_count, 2 * tok_count), 1)
    allowed = (columns <= rows + tok_count) & (key_ids_ref[...] == query_ids_ref[...])
    scores = jnp.where(allowed, dot(query, keys, across) * scale, -1e30)
    peak = jnp.max(scores, axis=-1, keepdims=True)
    raised = jnp.where(allowed, jnp.exp(scores - peak), 0.0)
    prob = raised / jnp.sum(raised, axis=-1, keepdims=True)
    prob_b = prob.astype(jnp.bfloat16)
    dprob = dot(upstream, values, across)
    delta = jnp.sum(prob * dprob, axis=-1, keepdims=True)
    dscore = (prob * (dprob - delta) * scale).astype(jnp.bfloat16)
    dk = dot(dscore, query, over)
    dv = dot(prob_b, upstream, over)
    back_ref[:, :heads] = dk[:tok_count].astype(jnp.bfloat16)
    back_ref[:, heads:] = dv[:tok_count].astype(jnp.bfloat16)
    own_ref[:, :heads] = dk[tok_count:]
    own_ref[:, heads:] = dv[tok_count:]
    dq_ref[...] = jnp.dot(dscore, keys, preferred_element_type=jnp.float32).astype(jnp.bfloat16)
    attn_ref[...] = jnp.dot(prob_b, values, preferred_element_type=jnp.float32).astype(jnp.bfloat16)


def term_kernel(core_ref, tok_ref, dq_ref, own_ref, back_ref, mine_ref, other_ref, grad_ref):
    first = core_ref[0] == 0
    heads = dq_ref.shape[1]
    grad_ref[:, :heads] = dq_ref[...]
    grad_ref[:, heads:] = (own_ref[...] + back_ref[...].astype(jnp.float32)).astype(jnp.bfloat16)
    grad = grad_ref[...]
    columns = grad.shape[1]
    low = lax.broadcasted_iota(jnp.int32, (8, 8, columns), 1) < 4
    for zh in range(4):
        for zl in range(2):
            for xlh in range(2):
                for xll in range(2):
                    f = fsdp_index(zh, zl, xlh, xll)
                    term = lax.dot_general(
                        tok_ref[:, f * 128 : (f + 1) * 128],
                        grad,
                        (((0,), (0,)), ((), ())),
                        preferred_element_type=jnp.float32,
                    )
                    by_hi = term.reshape(8, 2, 8, columns)
                    even, odd = by_hi[:, 0], by_hi[:, 1]
                    zero = jnp.where(low, even, pltpu.roll(odd, 4, 1))
                    one = jnp.where(low, pltpu.roll(even, 4, 1), odd)
                    mine = jnp.where(first, zero, one).reshape(4, 2, 8, columns)
                    other = jnp.where(first, one, zero).reshape(4, 2, 8, columns)
                    for yl in range(2):
                        at = (zl * 2 + xll) * 2 + yl, zh * 2 + xlh
                        mine_ref[at] = mine[:, yl].reshape(32, columns).astype(jnp.bfloat16)
                        other_ref[at] = other[:, yl].reshape(32, columns).astype(jnp.bfloat16)


def back_kernel(grad_ref, weight_ref, out_ref, *scratch):
    grad, count = grad_ref[...], 4
    parts, blocks, arrived, left = scratch[:4], scratch[4:8], scratch[8], scratch[9]
    rows = weight_ref.shape[0] // count
    fetches = [
        pltpu.make_async_copy(weight_ref.at[pl.ds(i * rows, rows), :], parts[i], arrived.at[i])
        for i in range(count)
    ]
    stores = [
        pltpu.make_async_copy(blocks[i], out_ref.at[:, pl.ds(i * rows, rows)], left.at[i])
        for i in range(count)
    ]
    for fetch in fetches:
        fetch.start()
    for i in range(count):
        fetches[i].wait()
        blocks[i][...] = lax.dot_general(
            grad, parts[i][...], (((1,), (1,)), ((), ())), preferred_element_type=jnp.float32
        ).astype(jnp.bfloat16)
        stores[i].start()
    for store in stores:
        store.wait()


def whole(memory=pltpu.VMEM):
    return pl.BlockSpec(memory_space=memory)


def call(kernel, outs, flops, moved, *args, far_args=(), far_outs=(), scratch=()):
    def space(i, array, far):
        return whole(pl.ANY if i in far else pltpu.SMEM if array.ndim == 1 else pltpu.VMEM)

    shapes = [jax.ShapeDtypeStruct(shape, dtype) for shape, dtype in outs]
    return pl.pallas_call(
        kernel,
        out_shape=shapes,
        in_specs=[space(i, arg, far_args) for i, arg in enumerate(args)],
        out_specs=[space(i, shape, far_outs) for i, shape in enumerate(shapes)],
        scratch_shapes=list(scratch),
        compiler_params=pltpu.CompilerParams(vmem_limit_bytes=VMEM),
        cost_estimate=pl.CostEstimate(flops=flops, bytes_accessed=moved, transcendentals=0),
    )(*args)


def local(tokens, segment_ids, w_query, w_key, w_value, grad_out):
    tok_rows = tokens[0]
    tok_count, depth = tok_rows.shape
    heads = w_query.shape[1]
    bf16, f32 = jnp.bfloat16, jnp.float32
    core = lax.axis_index("c")
    core_arg = core.reshape(1).astype(jnp.int32)
    flops, moved = 2 * tok_count * depth * 3 * heads, 3 * 2 * tok_count * depth

    weight_part = pltpu.VMEM((depth // 4, 3 * heads), bf16)
    tok_part = pltpu.VMEM((tok_count, depth // 4), bf16)

    local_weight = jnp.concatenate([w_query, w_key, w_value], axis=1)
    start = core * 64 + lax.axis_index("yl") * 32
    quarter = lax.dynamic_slice_in_dim(local_weight, start, 32, axis=0)
    far = lax.all_to_all(jnp.broadcast_to(quarter, (8,) + quarter.shape), ("zh", "xlh"), 0, 0)
    half = cube_exchange(jnp.broadcast_to(far, (8,) + far.shape))
    other_half = lax.ppermute(half, "c", SWAP)
    full_weight, qkv_rounded = call(
        project_kernel,
        [((depth, 3 * heads), bf16), ((tok_count, 3 * heads), bf16)],
        flops,
        moved,
        core_arg,
        tok_rows,
        half,
        other_half,
        far_outs=(0,),
        scratch=[weight_part] * 4 + [pltpu.SemaphoreType.DMA((4,))],
    )

    first_row = lax.axis_index(FSDP) * tok_count
    id_line = segment_ids[0]
    own_ids = lax.dynamic_slice_in_dim(id_line, first_row, tok_count)
    prior_ids = lax.dynamic_slice_in_dim(id_line, jnp.maximum(first_row - tok_count, 0), tok_count)
    prior_ids = jnp.where(first_row > 0, prior_ids, -1)
    attn, query_gradient, own_parts, back_parts = call(
        attend_kernel,
        [
            ((tok_count, heads), bf16),
            ((tok_count, heads), bf16),
            ((tok_count, 2 * heads), f32),
            ((tok_count, 2 * heads), bf16),
        ],
        7 * 4 * tok_count * tok_count * heads,
        12 * tok_count * heads,
        qkv_rounded,
        shifted(qkv_rounded[:, heads:], 1),
        own_ids[:, None],
        jnp.concatenate([prior_ids, own_ids])[None, :],
        grad_out[0],
    )
    returned = shifted(back_parts, -1)

    parts = (8, 8, 32, 3 * heads)
    mine, other, grad_proj = call(
        term_kernel,
        [(parts, bf16), (parts, bf16), ((tok_count, 3 * heads), bf16)],
        flops,
        moved,
        core_arg,
        tok_rows,
        query_gradient,
        own_parts,
        returned,
    )
    swapped = lax.ppermute(other, "c", SWAP)
    (grad_input,) = call(
        back_kernel,
        [((tok_count, depth), bf16)],
        flops,
        moved,
        grad_proj,
        full_weight,
        far_args=(1,),
        far_outs=(0,),
        scratch=[weight_part] * 4 + [tok_part] * 4 + [pltpu.SemaphoreType.DMA((4,))] * 2,
    )
    swapped, grad_input = lax.optimization_barrier((swapped, grad_input))
    chip = (mine.astype(jnp.float32) + swapped.astype(jnp.float32)).astype(jnp.bfloat16)
    cube = jnp.sum(cube_exchange(chip).astype(jnp.float32), axis=0)
    rows = cube.astype(jnp.bfloat16).reshape(64, 4, 3 * heads)
    rows = lax.all_to_all(rows, ("zh", "xlh", "yh", "xh"), 0, 0)
    count = math.prod(lax.axis_size(name) for name in FSDP + DP) * tok_count
    grads = jnp.sum(rows.astype(jnp.float32), axis=0) * (1.0 / math.sqrt(count))
    return (
        attn[None],
        grad_input[None],
        grads[:, :heads],
        grads[:, heads : 2 * heads],
        grads[:, 2 * heads :],
    )


def solution(mesh):
    fine = Mesh(mesh.devices.reshape(SIZES), FSDP + DP)
    rows = P(DP, FSDP, None)
    weight = P(FSDP, None)
    gradient = P(FSDP + DP, None)
    return jax.shard_map(
        local,
        mesh=fine,
        in_specs=(rows, P(DP, None), weight, weight, weight, rows),
        out_specs=(rows, rows, gradient, gradient, gradient),
        check_vma=False,
    )
```

```python
import math

import jax
import jax.numpy as jnp
from jax import lax
from jax.experimental import pallas as pl
from jax.experimental.pallas import tpu as pltpu
from jax.sharding import Mesh
from jax.sharding import PartitionSpec as P

FSDP = ("zh", "zl", "xlh", "xll")
DP = ("yh", "yl", "xh", "c")
SIZES = (4, 2, 2, 2, 4, 2, 2, 2)
SWAP = [(0, 1), (1, 0)]
VMEM = 20 * 1024 * 1024


def fsdp_index(zh, zl, xlh, xll):
    return ((zh * 2 + zl) * 2 + xlh) * 2 + xll


def cubes():
    def index(z, x, y, core):
        x_hi = x // 4
        fsdp = z * 4 + x % 4
        return ((fsdp * 8 + y) * 2 + x_hi) * 2 + core

    groups = []
    for core in range(2):
        for corner in range(64):
            low = [2 * (corner // 16) + core, 2 * (corner // 4 % 4) + core, 2 * (corner % 4) + core]
            members = []
            for bits in range(8):
                want = (bits // 4, bits // 2 % 2, bits % 2)
                z, x, y = ((a + (a + b) % 2) % 8 for a, b in zip(low, want))
                members.append(index(z, x, y, core))
            groups.append(members)
    return groups


def cube_exchange(block):
    return lax.all_to_all(block, FSDP + DP, 0, 0, axis_index_groups=cubes())


def shifted(block, distance):
    route = [(i - distance, i) for i in range(32) if 0 <= i - distance < 32]
    return lax.ppermute(block, FSDP, route)


def project_kernel(core_ref, tok_ref, mine_ref, other_ref, weight_ref, qkv_ref, *scratch):
    core = core_ref[0]
    total, copies = None, []
    for zh in range(4):
        part_ref, done = scratch[zh], scratch[4].at[zh]
        for zl in range(2):
            for xlh in range(2):
                for xll in range(2):
                    for yl in range(2):
                        row = fsdp_index(0, zl, xlh, xll) * 128 + yl * 32
                        at = (zl * 2 + xll) * 2 + yl, zh * 2 + xlh
                        here = pl.multiple_of(row + core * 64, 32)
                        there = pl.multiple_of(row + (1 - core) * 64, 32)
                        part_ref[pl.ds(here, 32), :] = mine_ref[at]
                        part_ref[pl.ds(there, 32), :] = other_ref[at]
        rows = part_ref.shape[0]
        copy = pltpu.make_async_copy(part_ref, weight_ref.at[pl.ds(zh * rows, rows), :], done)
        copy.start()
        copies.append(copy)
        term = jnp.dot(
            tok_ref[:, zh * rows : (zh + 1) * rows], part_ref[...], preferred_element_type=jnp.float32
        )
        total = term if total is None else total + term
    qkv_ref[...] = total.astype(jnp.bfloat16)
    for copy in copies:
        copy.wait()


def attend_kernel(
    core_ref,
    tok_ref,
    qkv_ref,
    earlier_ref,
    later_ref,
    prior_ids_ref,
    ids_ref,
    next_ids_ref,
    upstream_ref,
    attn_ref,
    grad_ref,
    mine_ref,
    other_ref,
    tok_rows,
    tok_here,
):
    fetch = pltpu.make_async_copy(tok_ref, tok_rows, tok_here)
    fetch.start()
    tok_count, heads = attn_ref.shape
    scale = 1.0 / math.sqrt(heads)
    across, over = (((1,), (1,)), ((), ())), (((0,), (0,)), ((), ()))
    rows = lax.broadcasted_iota(jnp.int32, (tok_count, 2 * tok_count), 0)
    columns = lax.broadcasted_iota(jnp.int32, (tok_count, 2 * tok_count), 1)
    causal = columns <= rows + tok_count
    diagonal = rows[:, :tok_count] == columns[:, :tok_count]
    prior_ids, own_ids, next_ids = (
        ref[...].astype(jnp.float32) for ref in (prior_ids_ref, ids_ref, next_ids_ref)
    )

    def dot(a, b, dims):
        return lax.dot_general(a, b, dims, preferred_element_type=jnp.float32)

    def attend(query, keys, values, upstream, before, ids):
        query_ids = jnp.sum(jnp.where(diagonal, ids, 0.0), axis=1, keepdims=True)
        allowed = causal & (jnp.concatenate([before, ids], axis=1) == query_ids)
        scores = jnp.where(allowed, dot(query, keys, across) * scale, -1e30)
        peak = jnp.max(scores, axis=-1, keepdims=True)
        raised = jnp.where(allowed, jnp.exp(scores - peak), 0.0)
        prob = raised / jnp.sum(raised, axis=-1, keepdims=True)
        dprob = dot(upstream, values, across)
        delta = jnp.sum(prob * dprob, axis=-1, keepdims=True)
        dscore = (prob * (dprob - delta) * scale).astype(jnp.bfloat16)
        return prob.astype(jnp.bfloat16), dscore

    query, upstream = qkv_ref[:, :heads], upstream_ref[...]
    own_keys, own_values = qkv_ref[:, heads : 2 * heads], qkv_ref[:, 2 * heads :]
    keys = jnp.concatenate([earlier_ref[:, :heads], own_keys], axis=0)
    values = jnp.concatenate([earlier_ref[:, heads:], own_values], axis=0)
    prob_b, dscore = attend(query, keys, values, upstream, prior_ids, own_ids)
    attn_ref[...] = jnp.dot(prob_b, values, preferred_element_type=jnp.float32).astype(jnp.bfloat16)
    dq = jnp.dot(dscore, keys, preferred_element_type=jnp.float32)

    later_query, later_upstream = later_ref[:, :heads], later_ref[:, 3 * heads :]
    keys = jnp.concatenate([own_keys, later_ref[:, heads : 2 * heads]], axis=0)
    values = jnp.concatenate([own_values, later_ref[:, 2 * heads : 3 * heads]], axis=0)
    later_prob_b, later_dscore = attend(
        later_query, keys, values, later_upstream, own_ids, next_ids
    )
    dk = dot(dscore, query, over)[tok_count:] + dot(later_dscore, later_query, over)[:tok_count]
    dv = dot(prob_b, upstream, over)[tok_count:] + dot(later_prob_b, later_upstream, over)[:tok_count]
    for i, grad in enumerate((dq, dk, dv)):
        grad_ref[:, i * heads : (i + 1) * heads] = grad.astype(jnp.bfloat16)

    fetch.wait()
    first = core_ref[0] == 0
    grad = grad_ref[...]
    width = grad.shape[1]
    low = lax.broadcasted_iota(jnp.int32, (8, 8, width), 1) < 4
    for zh in range(4):
        for zl in range(2):
            for xlh in range(2):
                for xll in range(2):
                    f = fsdp_index(zh, zl, xlh, xll)
                    term = lax.dot_general(
                        tok_rows[:, f * 128 : (f + 1) * 128],
                        grad,
                        (((0,), (0,)), ((), ())),
                        preferred_element_type=jnp.float32,
                    )
                    by_hi = term.reshape(8, 2, 8, width)
                    even, odd = by_hi[:, 0], by_hi[:, 1]
                    zero = jnp.where(low, even, pltpu.roll(odd, 4, 1))
                    one = jnp.where(low, pltpu.roll(even, 4, 1), odd)
                    mine = jnp.where(first, zero, one).reshape(4, 2, 8, width)
                    other = jnp.where(first, one, zero).reshape(4, 2, 8, width)
                    for yl in range(2):
                        at = (zl * 2 + xll) * 2 + yl, zh * 2 + xlh
                        mine_ref[at] = mine[:, yl].reshape(32, width).astype(jnp.bfloat16)
                        other_ref[at] = other[:, yl].reshape(32, width).astype(jnp.bfloat16)


def back_kernel(grad_ref, weight_ref, out_ref, *scratch):
    grad, count = grad_ref[...], 4
    parts, blocks, arrived, left = scratch[:4], scratch[4:8], scratch[8], scratch[9]
    rows = weight_ref.shape[0] // count
    fetches = [
        pltpu.make_async_copy(weight_ref.at[pl.ds(i * rows, rows), :], parts[i], arrived.at[i])
        for i in range(count)
    ]
    stores = [
        pltpu.make_async_copy(blocks[i], out_ref.at[:, pl.ds(i * rows, rows)], left.at[i])
        for i in range(count)
    ]
    for fetch in fetches:
        fetch.start()
    for i in range(count):
        fetches[i].wait()
        blocks[i][...] = lax.dot_general(
            grad, parts[i][...], (((1,), (1,)), ((), ())), preferred_element_type=jnp.float32
        ).astype(jnp.bfloat16)
        stores[i].start()
    for store in stores:
        store.wait()


def whole(memory=pltpu.VMEM):
    return pl.BlockSpec(memory_space=memory)


def call(kernel, outs, flops, moved, *args, far_args=(), far_outs=(), scratch=()):
    def space(i, array, far):
        return whole(pltpu.HBM if i in far else pltpu.SMEM if array.ndim == 1 else pltpu.VMEM)

    shapes = [jax.ShapeDtypeStruct(shape, dtype) for shape, dtype in outs]
    return pl.pallas_call(
        kernel,
        out_shape=shapes,
        in_specs=[space(i, arg, far_args) for i, arg in enumerate(args)],
        out_specs=[space(i, shape, far_outs) for i, shape in enumerate(shapes)],
        scratch_shapes=list(scratch),
        compiler_params=pltpu.CompilerParams(vmem_limit_bytes=VMEM),
        cost_estimate=pl.CostEstimate(flops=flops, bytes_accessed=moved, transcendentals=0),
    )(*args)


def local(tokens, segment_ids, w_query, w_key, w_value, grad_out):
    tok_rows = tokens[0]
    tok_count, depth = tok_rows.shape
    heads = w_query.shape[1]
    bf16 = jnp.bfloat16
    core = lax.axis_index("c")
    core_arg = core.reshape(1).astype(jnp.int32)
    flops, moved = 2 * tok_count * depth * 3 * heads, 3 * 2 * tok_count * depth

    weight_part = pltpu.VMEM((depth // 4, 3 * heads), bf16)
    tok_part = pltpu.VMEM((tok_count, depth // 4), bf16)

    local_weight = jnp.concatenate([w_query, w_key, w_value], axis=1)
    start = core * 64 + lax.axis_index("yl") * 32
    quarter = lax.dynamic_slice_in_dim(local_weight, start, 32, axis=0)
    far = lax.all_to_all(jnp.broadcast_to(quarter, (8,) + quarter.shape), ("zh", "xlh"), 0, 0)
    half = cube_exchange(jnp.broadcast_to(far, (8,) + far.shape))
    other_half = lax.ppermute(half, "c", SWAP)
    full_weight, qkv_rounded = call(
        project_kernel,
        [((depth, 3 * heads), bf16), ((tok_count, 3 * heads), bf16)],
        flops,
        moved,
        core_arg,
        tok_rows,
        half,
        other_half,
        far_outs=(0,),
        scratch=[weight_part] * 4 + [pltpu.SemaphoreType.DMA((4,))],
    )

    device = lax.axis_index(FSDP)
    prior_ids, own_ids, next_ids = (
        lax.dynamic_slice_in_dim(segment_ids, jnp.clip(device + i, 0, 31) * tok_count, tok_count, axis=1)
        for i in (-1, 0, 1)
    )
    prior_ids = jnp.where(device > 0, prior_ids, -1)
    next_ids = jnp.where(device < 31, next_ids, -2)
    earlier = shifted(qkv_rounded[:, heads:], 1)
    later = shifted(jnp.concatenate([qkv_rounded, grad_out[0]], axis=1), -1)
    parts = (8, 8, 32, 3 * heads)
    attn, grad_proj, mine, other = call(
        attend_kernel,
        [
            ((tok_count, heads), bf16),
            ((tok_count, 3 * heads), bf16),
            (parts, bf16),
            (parts, bf16),
        ],
        flops + 14 * 4 * tok_count * tok_count * heads,
        moved,
        core_arg,
        pltpu.with_memory_space_constraint(tok_rows, pltpu.HBM),
        qkv_rounded,
        earlier,
        later,
        prior_ids,
        own_ids,
        next_ids,
        grad_out[0],
        far_args=(1,),
        scratch=[pltpu.VMEM((tok_count, depth), bf16), pltpu.SemaphoreType.DMA],
    )
    swapped = lax.ppermute(other, "c", SWAP)
    (grad_input,) = call(
        back_kernel,
        [((tok_count, depth), bf16)],
        flops,
        moved,
        grad_proj,
        full_weight,
        far_args=(1,),
        far_outs=(0,),
        scratch=[weight_part] * 4 + [tok_part] * 4 + [pltpu.SemaphoreType.DMA((4,))] * 2,
    )
    swapped, grad_input = lax.optimization_barrier((swapped, grad_input))
    chip = (mine.astype(jnp.float32) + swapped.astype(jnp.float32)).astype(jnp.bfloat16)
    cube = jnp.sum(cube_exchange(chip).astype(jnp.float32), axis=0)
    rows = cube.astype(jnp.bfloat16).reshape(64, 4, 3 * heads)
    rows = lax.all_to_all(rows, ("zh", "xlh", "yh", "xh"), 0, 0)
    count = math.prod(lax.axis_size(name) for name in FSDP + DP) * tok_count
    grads = jnp.sum(rows.astype(jnp.float32), axis=0) * (1.0 / math.sqrt(count))
    return (
        attn[None],
        grad_input[None],
        grads[:, :heads],
        grads[:, heads : 2 * heads],
        grads[:, 2 * heads :],
    )


def solution(mesh):
    fine = Mesh(mesh.devices.reshape(SIZES), FSDP + DP)
    rows = P(DP, FSDP, None)
    weight = P(FSDP, None)
    gradient = P(FSDP + DP, None)
    return jax.shard_map(
        local,
        mesh=fine,
        in_specs=(rows, P(DP, None), weight, weight, weight, rows),
        out_specs=(rows, rows, gradient, gradient, gradient),
        check_vma=False,
    )
```

```python
import math

import jax
import jax.numpy as jnp
from jax import lax
from jax.experimental import pallas as pl
from jax.experimental.pallas import tpu as pltpu
from jax.sharding import Mesh
from jax.sharding import PartitionSpec as P

FSDP = ("zh", "zl", "xlh", "xll")
DP = ("yh", "yl", "xh", "c")
SIZES = (4, 2, 2, 2, 4, 2, 2, 2)
SWAP = [(0, 1), (1, 0)]
VMEM = 20 * 1024 * 1024


def fsdp_index(zh, zl, xlh, xll):
    return ((zh * 2 + zl) * 2 + xlh) * 2 + xll


def cubes():
    def index(z, x, y, core):
        x_hi = x // 4
        fsdp = z * 4 + x % 4
        return ((fsdp * 8 + y) * 2 + x_hi) * 2 + core

    groups = []
    for core in range(2):
        for corner in range(64):
            low = [2 * (corner // 16) + core, 2 * (corner // 4 % 4) + core, 2 * (corner % 4) + core]
            members = []
            for bits in range(8):
                want = (bits // 4, bits // 2 % 2, bits % 2)
                z, x, y = ((a + (a + b) % 2) % 8 for a, b in zip(low, want))
                members.append(index(z, x, y, core))
            groups.append(members)
    return groups


def cube_exchange(block):
    return lax.all_to_all(block, FSDP + DP, 0, 0, axis_index_groups=cubes())


def shifted(block, distance):
    route = [(i - distance, i) for i in range(32) if 0 <= i - distance < 32]
    return lax.ppermute(block, FSDP, route)


def project_kernel(
    core_ref, tok_ref, mine_ref, other_ref, upstream_ref, weight_ref, sent_ref, *scratch
):
    heads = upstream_ref.shape[1]
    sent_ref[:, 3 * heads :] = upstream_ref[...]
    core = core_ref[0]
    total, copies = None, []
    for zh in range(4):
        part_ref, done = scratch[zh], scratch[4].at[zh]
        for zl in range(2):
            for xlh in range(2):
                for xll in range(2):
                    for yl in range(2):
                        row = fsdp_index(0, zl, xlh, xll) * 128 + yl * 32
                        at = (zl * 2 + xll) * 2 + yl, zh * 2 + xlh
                        here = pl.multiple_of(row + core * 64, 32)
                        there = pl.multiple_of(row + (1 - core) * 64, 32)
                        part_ref[pl.ds(here, 32), :] = mine_ref[at]
                        part_ref[pl.ds(there, 32), :] = other_ref[at]
        rows = part_ref.shape[0]
        copy = pltpu.make_async_copy(part_ref, weight_ref.at[pl.ds(zh * rows, rows), :], done)
        copy.start()
        copies.append(copy)
        term = jnp.dot(
            tok_ref[:, zh * rows : (zh + 1) * rows], part_ref[...], preferred_element_type=jnp.float32
        )
        total = term if total is None else total + term
    sent_ref[:, : 3 * heads] = total.astype(jnp.bfloat16)
    for copy in copies:
        copy.wait()


def attend_kernel(
    core_ref,
    tok_ref,
    sent_ref,
    earlier_ref,
    later_ref,
    prior_ids_ref,
    ids_ref,
    next_ids_ref,
    attn_ref,
    grad_ref,
    mine_ref,
    other_ref,
    tok_rows,
    tok_here,
):
    fetch = pltpu.make_async_copy(tok_ref, tok_rows, tok_here)
    fetch.start()
    tok_count, heads = attn_ref.shape
    scale = 1.0 / math.sqrt(heads)
    across, over = (((1,), (1,)), ((), ())), (((0,), (0,)), ((), ()))
    rows = lax.broadcasted_iota(jnp.int32, (tok_count, 2 * tok_count), 0)
    columns = lax.broadcasted_iota(jnp.int32, (tok_count, 2 * tok_count), 1)
    causal = columns <= rows + tok_count
    diagonal = rows[:, :tok_count] == columns[:, :tok_count]
    prior_ids, own_ids, next_ids = (
        ref[...].astype(jnp.float32) for ref in (prior_ids_ref, ids_ref, next_ids_ref)
    )

    def dot(a, b, dims):
        return lax.dot_general(a, b, dims, preferred_element_type=jnp.float32)

    def attend(query, keys, values, upstream, before, ids):
        query_ids = jnp.sum(jnp.where(diagonal, ids, 0.0), axis=1, keepdims=True)
        allowed = causal & (jnp.concatenate([before, ids], axis=1) == query_ids)
        scores = jnp.where(allowed, dot(query, keys, across) * scale, -1e30)
        peak = jnp.max(scores, axis=-1, keepdims=True)
        raised = jnp.where(allowed, jnp.exp(scores - peak), 0.0)
        prob = raised / jnp.sum(raised, axis=-1, keepdims=True)
        dprob = dot(upstream, values, across)
        delta = jnp.sum(prob * dprob, axis=-1, keepdims=True)
        dscore = (prob * (dprob - delta) * scale).astype(jnp.bfloat16)
        return prob.astype(jnp.bfloat16), dscore

    query, upstream = sent_ref[:, :heads], sent_ref[:, 3 * heads :]
    own_keys, own_values = sent_ref[:, heads : 2 * heads], sent_ref[:, 2 * heads : 3 * heads]
    keys = jnp.concatenate([earlier_ref[:, :heads], own_keys], axis=0)
    values = jnp.concatenate([earlier_ref[:, heads:], own_values], axis=0)
    prob_b, dscore = attend(query, keys, values, upstream, prior_ids, own_ids)
    attn_ref[...] = jnp.dot(prob_b, values, preferred_element_type=jnp.float32).astype(jnp.bfloat16)
    dq = jnp.dot(dscore, keys, preferred_element_type=jnp.float32)

    later_query, later_upstream = later_ref[:, :heads], later_ref[:, 3 * heads :]
    keys = jnp.concatenate([own_keys, later_ref[:, heads : 2 * heads]], axis=0)
    values = jnp.concatenate([own_values, later_ref[:, 2 * heads : 3 * heads]], axis=0)
    later_prob_b, later_dscore = attend(
        later_query, keys, values, later_upstream, own_ids, next_ids
    )
    dk = dot(dscore, query, over)[tok_count:] + dot(later_dscore, later_query, over)[:tok_count]
    dv = dot(prob_b, upstream, over)[tok_count:] + dot(later_prob_b, later_upstream, over)[:tok_count]
    for i, grad in enumerate((dq, dk, dv)):
        grad_ref[:, i * heads : (i + 1) * heads] = grad.astype(jnp.bfloat16)

    fetch.wait()
    first = core_ref[0] == 0
    grad = grad_ref[...]
    width = grad.shape[1]
    low = lax.broadcasted_iota(jnp.int32, (8, 8, width), 1) < 4
    for zh in range(4):
        for zl in range(2):
            for xlh in range(2):
                for xll in range(2):
                    f = fsdp_index(zh, zl, xlh, xll)
                    term = lax.dot_general(
                        tok_rows[:, f * 128 : (f + 1) * 128],
                        grad,
                        (((0,), (0,)), ((), ())),
                        preferred_element_type=jnp.float32,
                    )
                    by_hi = term.reshape(8, 2, 8, width)
                    even, odd = by_hi[:, 0], by_hi[:, 1]
                    zero = jnp.where(low, even, pltpu.roll(odd, 4, 1))
                    one = jnp.where(low, pltpu.roll(even, 4, 1), odd)
                    mine = jnp.where(first, zero, one).reshape(4, 2, 8, width)
                    other = jnp.where(first, one, zero).reshape(4, 2, 8, width)
                    for yl in range(2):
                        at = (zl * 2 + xll) * 2 + yl, zh * 2 + xlh
                        mine_ref[at] = mine[:, yl].reshape(32, width).astype(jnp.bfloat16)
                        other_ref[at] = other[:, yl].reshape(32, width).astype(jnp.bfloat16)


def back_kernel(grad_ref, weight_ref, out_ref, *scratch):
    grad, count = grad_ref[...], 4
    parts, blocks, arrived, left = scratch[:4], scratch[4:8], scratch[8], scratch[9]
    rows = weight_ref.shape[0] // count
    fetches = [
        pltpu.make_async_copy(weight_ref.at[pl.ds(i * rows, rows), :], parts[i], arrived.at[i])
        for i in range(count)
    ]
    stores = [
        pltpu.make_async_copy(blocks[i], out_ref.at[:, pl.ds(i * rows, rows)], left.at[i])
        for i in range(count)
    ]
    for fetch in fetches:
        fetch.start()
    for i in range(count):
        fetches[i].wait()
        blocks[i][...] = lax.dot_general(
            grad, parts[i][...], (((1,), (1,)), ((), ())), preferred_element_type=jnp.float32
        ).astype(jnp.bfloat16)
        stores[i].start()
    for store in stores:
        store.wait()


def whole(memory=pltpu.VMEM):
    return pl.BlockSpec(memory_space=memory)


def call(kernel, outs, flops, moved, *args, far_args=(), far_outs=(), scratch=()):
    def space(i, array, far):
        return whole(pltpu.HBM if i in far else pltpu.SMEM if array.ndim == 1 else pltpu.VMEM)

    shapes = [jax.ShapeDtypeStruct(shape, dtype) for shape, dtype in outs]
    return pl.pallas_call(
        kernel,
        out_shape=shapes,
        in_specs=[space(i, arg, far_args) for i, arg in enumerate(args)],
        out_specs=[space(i, shape, far_outs) for i, shape in enumerate(shapes)],
        scratch_shapes=list(scratch),
        compiler_params=pltpu.CompilerParams(vmem_limit_bytes=VMEM),
        cost_estimate=pl.CostEstimate(flops=flops, bytes_accessed=moved, transcendentals=0),
    )(*args)


def local(tokens, segment_ids, w_query, w_key, w_value, grad_out):
    tok_rows = tokens[0]
    tok_count, depth = tok_rows.shape
    heads = w_query.shape[1]
    bf16 = jnp.bfloat16
    core = lax.axis_index("c")
    core_arg = core.reshape(1).astype(jnp.int32)
    flops, moved = 2 * tok_count * depth * 3 * heads, 3 * 2 * tok_count * depth

    weight_part = pltpu.VMEM((depth // 4, 3 * heads), bf16)
    tok_part = pltpu.VMEM((tok_count, depth // 4), bf16)

    local_weight = jnp.concatenate([w_query, w_key, w_value], axis=1)
    start = core * 64 + lax.axis_index("yl") * 32
    quarter = lax.dynamic_slice_in_dim(local_weight, start, 32, axis=0)
    far = lax.all_to_all(jnp.broadcast_to(quarter, (8,) + quarter.shape), ("zh", "xlh"), 0, 0)
    half = cube_exchange(jnp.broadcast_to(far, (8,) + far.shape))
    other_half = lax.ppermute(half, "c", SWAP)
    full_weight, sent = call(
        project_kernel,
        [((depth, 3 * heads), bf16), ((tok_count, 4 * heads), bf16)],
        flops,
        moved,
        core_arg,
        tok_rows,
        half,
        other_half,
        grad_out[0],
        far_outs=(0,),
        scratch=[weight_part] * 4 + [pltpu.SemaphoreType.DMA((4,))],
    )

    device = lax.axis_index(FSDP)
    prior_ids, own_ids, next_ids = (
        lax.dynamic_slice_in_dim(segment_ids, jnp.clip(device + i, 0, 31) * tok_count, tok_count, axis=1)
        for i in (-1, 0, 1)
    )
    prior_ids = jnp.where(device > 0, prior_ids, -1)
    next_ids = jnp.where(device < 31, next_ids, -2)
    earlier = shifted(sent[:, heads : 3 * heads], 1)
    later = shifted(sent, -1)
    parts = (8, 8, 32, 3 * heads)
    attn, grad_proj, mine, other = call(
        attend_kernel,
        [
            ((tok_count, heads), bf16),
            ((tok_count, 3 * heads), bf16),
            (parts, bf16),
            (parts, bf16),
        ],
        flops + 14 * 4 * tok_count * tok_count * heads,
        moved,
        core_arg,
        pltpu.with_memory_space_constraint(tok_rows, pltpu.HBM),
        sent,
        earlier,
        later,
        prior_ids,
        own_ids,
        next_ids,
        far_args=(1,),
        scratch=[pltpu.VMEM((tok_count, depth), bf16), pltpu.SemaphoreType.DMA],
    )
    swapped = lax.ppermute(other, "c", SWAP)
    (grad_input,) = call(
        back_kernel,
        [((tok_count, depth), bf16)],
        flops,
        moved,
        grad_proj,
        full_weight,
        far_args=(1,),
        far_outs=(0,),
        scratch=[weight_part] * 4 + [tok_part] * 4 + [pltpu.SemaphoreType.DMA((4,))] * 2,
    )
    swapped, grad_input = lax.optimization_barrier((swapped, grad_input))
    chip = (mine.astype(jnp.float32) + swapped.astype(jnp.float32)).astype(jnp.bfloat16)
    cube = jnp.sum(cube_exchange(chip).astype(jnp.float32), axis=0)
    rows = cube.astype(jnp.bfloat16).reshape(64, 4, 3 * heads)
    rows = lax.all_to_all(rows, ("zh", "xlh", "yh", "xh"), 0, 0)
    count = math.prod(lax.axis_size(name) for name in FSDP + DP) * tok_count
    grads = jnp.sum(rows.astype(jnp.float32), axis=0) * (1.0 / math.sqrt(count))
    return (
        attn[None],
        grad_input[None],
        grads[:, :heads],
        grads[:, heads : 2 * heads],
        grads[:, 2 * heads :],
    )


def solution(mesh):
    fine = Mesh(mesh.devices.reshape(SIZES), FSDP + DP)
    rows = P(DP, FSDP, None)
    weight = P(FSDP, None)
    gradient = P(FSDP + DP, None)
    return jax.shard_map(
        local,
        mesh=fine,
        in_specs=(rows, P(DP, None), weight, weight, weight, rows),
        out_specs=(rows, rows, gradient, gradient, gradient),
        check_vma=False,
    )
```

```python
import math

import jax
import jax.numpy as jnp
from jax import lax
from jax.experimental import pallas as pl
from jax.experimental.pallas import tpu as pltpu
from jax.sharding import Mesh
from jax.sharding import PartitionSpec as P

FSDP = ("zh", "zl", "xlh", "xll")
DP = ("yh", "yl", "xh", "c")
SIZES = (4, 2, 2, 2, 4, 2, 2, 2)
SWAP = [(0, 1), (1, 0)]
VMEM = 20 * 1024 * 1024


def fsdp_index(zh, zl, xlh, xll):
    return ((zh * 2 + zl) * 2 + xlh) * 2 + xll


def cubes():
    def index(z, x, y, core):
        x_hi = x // 4
        fsdp = z * 4 + x % 4
        return ((fsdp * 8 + y) * 2 + x_hi) * 2 + core

    groups = []
    for core in range(2):
        for corner in range(64):
            low = [2 * (corner // 16) + core, 2 * (corner // 4 % 4) + core, 2 * (corner % 4) + core]
            members = []
            for bits in range(8):
                want = (bits // 4, bits // 2 % 2, bits % 2)
                z, x, y = ((a + (a + b) % 2) % 8 for a, b in zip(low, want))
                members.append(index(z, x, y, core))
            groups.append(members)
    return groups


def cube_exchange(block):
    return lax.all_to_all(block, FSDP + DP, 0, 0, axis_index_groups=cubes())


def shifted(block, distance):
    route = [(i - distance, i) for i in range(32) if 0 <= i - distance < 32]
    return lax.ppermute(block, FSDP, route)


def spread_kernel(start_ref, query_ref, key_ref, value_ref, out_ref, held, done):
    start = pl.multiple_of(start_ref[0], 32)
    copies = [
        pltpu.make_async_copy(ref.at[pl.ds(start, 32), :], held.at[i], done.at[i])
        for i, ref in enumerate((query_ref, key_ref, value_ref))
    ]
    for copy in copies:
        copy.start()
    for i, copy in enumerate(copies):
        copy.wait()
        for peer in range(out_ref.shape[0]):
            out_ref[peer, :, i * 128 : (i + 1) * 128] = held[i]


def project_kernel(
    core_ref, tok_ref, mine_ref, other_ref, upstream_ref, weight_ref, sent_ref, *scratch
):
    heads = upstream_ref.shape[1]
    sent_ref[:, 3 * heads :] = upstream_ref[...]
    core = core_ref[0]
    total, copies = None, []
    for zh in range(4):
        part_ref, done = scratch[zh], scratch[4].at[zh]
        for zl in range(2):
            for xlh in range(2):
                for xll in range(2):
                    for yl in range(2):
                        row = fsdp_index(0, zl, xlh, xll) * 128 + yl * 32
                        at = (zl * 2 + xll) * 2 + yl, zh * 2 + xlh
                        here = pl.multiple_of(row + core * 64, 32)
                        there = pl.multiple_of(row + (1 - core) * 64, 32)
                        part_ref[pl.ds(here, 32), :] = mine_ref[at]
                        part_ref[pl.ds(there, 32), :] = other_ref[at]
        rows = part_ref.shape[0]
        copy = pltpu.make_async_copy(part_ref, weight_ref.at[pl.ds(zh * rows, rows), :], done)
        copy.start()
        copies.append(copy)
        term = jnp.dot(
            tok_ref[:, zh * rows : (zh + 1) * rows], part_ref[...], preferred_element_type=jnp.float32
        )
        total = term if total is None else total + term
    sent_ref[:, : 3 * heads] = total.astype(jnp.bfloat16)
    for copy in copies:
        copy.wait()


def attend_kernel(
    core_ref,
    tok_ref,
    sent_ref,
    earlier_ref,
    later_ref,
    prior_ids_ref,
    ids_ref,
    next_ids_ref,
    attn_ref,
    grad_ref,
    mine_ref,
    other_ref,
    tok_rows,
    tok_here,
):
    fetch = pltpu.make_async_copy(tok_ref, tok_rows, tok_here)
    fetch.start()
    tok_count, heads = attn_ref.shape
    scale = 1.0 / math.sqrt(heads)
    across, over = (((1,), (1,)), ((), ())), (((0,), (0,)), ((), ()))
    rows = lax.broadcasted_iota(jnp.int32, (tok_count, 2 * tok_count), 0)
    columns = lax.broadcasted_iota(jnp.int32, (tok_count, 2 * tok_count), 1)
    diagonal = rows[:, :tok_count] == columns[:, :tok_count]
    prior_ids, own_ids, next_ids = (
        ref[...].astype(jnp.float32) for ref in (prior_ids_ref, ids_ref, next_ids_ref)
    )

    def dot(a, b, dims):
        return lax.dot_general(a, b, dims, preferred_element_type=jnp.float32)

    def attend(query, keys, values, upstream, causal, ids, key_ids):
        query_ids = jnp.sum(jnp.where(diagonal, ids, 0.0), axis=1, keepdims=True)
        allowed = causal & (jnp.concatenate(key_ids, axis=1) == query_ids)
        scores = jnp.where(allowed, dot(query, keys, across) * scale, -1e30)
        peak = jnp.max(scores, axis=-1, keepdims=True)
        raised = jnp.where(allowed, jnp.exp(scores - peak), 0.0)
        prob = raised / jnp.sum(raised, axis=-1, keepdims=True)
        dprob = dot(upstream, values, across)
        delta = jnp.sum(prob * dprob, axis=-1, keepdims=True)
        dscore = (prob * (dprob - delta) * scale).astype(jnp.bfloat16)
        return prob.astype(jnp.bfloat16), dscore

    query, upstream = sent_ref[:, :heads], sent_ref[:, 3 * heads :]
    own_keys, own_values = sent_ref[:, heads : 2 * heads], sent_ref[:, 2 * heads : 3 * heads]
    keys = jnp.concatenate([own_keys, earlier_ref[:, :heads]], axis=0)
    values = jnp.concatenate([own_values, earlier_ref[:, heads:]], axis=0)
    causal = (columns <= rows) | (columns >= tok_count)
    prob_b, dscore = attend(query, keys, values, upstream, causal, own_ids, [own_ids, prior_ids])
    attn_ref[...] = jnp.dot(prob_b, values, preferred_element_type=jnp.float32).astype(jnp.bfloat16)
    dq = jnp.dot(dscore, keys, preferred_element_type=jnp.float32)

    later_query, later_upstream = later_ref[:, :heads], later_ref[:, 3 * heads :]
    keys = jnp.concatenate([own_keys, later_ref[:, heads : 2 * heads]], axis=0)
    values = jnp.concatenate([own_values, later_ref[:, 2 * heads : 3 * heads]], axis=0)
    causal = columns <= rows + tok_count
    later_prob_b, later_dscore = attend(
        later_query, keys, values, later_upstream, causal, next_ids, [own_ids, next_ids]
    )
    dk = dot(dscore[:, :tok_count], query, over) + dot(later_dscore[:, :tok_count], later_query, over)
    dv = dot(prob_b[:, :tok_count], upstream, over) + dot(later_prob_b[:, :tok_count], later_upstream, over)
    for i, grad in enumerate((dq, dk, dv)):
        grad_ref[:, i * heads : (i + 1) * heads] = grad.astype(jnp.bfloat16)

    fetch.wait()
    first = core_ref[0] == 0
    grad = grad_ref[...]
    width = grad.shape[1]
    low = lax.broadcasted_iota(jnp.int32, (8, 8, width), 1) < 4
    for zh in range(4):
        for zl in range(2):
            for xlh in range(2):
                for xll in range(2):
                    f = fsdp_index(zh, zl, xlh, xll)
                    term = lax.dot_general(
                        tok_rows[:, f * 128 : (f + 1) * 128],
                        grad,
                        (((0,), (0,)), ((), ())),
                        preferred_element_type=jnp.float32,
                    )
                    by_hi = term.reshape(8, 2, 8, width)
                    even, odd = by_hi[:, 0], by_hi[:, 1]
                    zero = jnp.where(low, even, pltpu.roll(odd, 4, 1))
                    one = jnp.where(low, pltpu.roll(even, 4, 1), odd)
                    mine = jnp.where(first, zero, one).reshape(4, 2, 8, width)
                    other = jnp.where(first, one, zero).reshape(4, 2, 8, width)
                    for yl in range(2):
                        at = (zl * 2 + xll) * 2 + yl, zh * 2 + xlh
                        mine_ref[at] = mine[:, yl].reshape(32, width).astype(jnp.bfloat16)
                        other_ref[at] = other[:, yl].reshape(32, width).astype(jnp.bfloat16)


def back_kernel(grad_ref, weight_ref, out_ref, *scratch):
    grad, count = grad_ref[...], 4
    parts, blocks, arrived, left = scratch[:4], scratch[4:8], scratch[8], scratch[9]
    rows = weight_ref.shape[0] // count
    fetches = [
        pltpu.make_async_copy(weight_ref.at[pl.ds(i * rows, rows), :], parts[i], arrived.at[i])
        for i in range(count)
    ]
    stores = [
        pltpu.make_async_copy(blocks[i], out_ref.at[:, pl.ds(i * rows, rows)], left.at[i])
        for i in range(count)
    ]
    for fetch in fetches:
        fetch.start()
    for i in range(count):
        fetches[i].wait()
        blocks[i][...] = lax.dot_general(
            grad, parts[i][...], (((1,), (1,)), ((), ())), preferred_element_type=jnp.float32
        ).astype(jnp.bfloat16)
        stores[i].start()
    for store in stores:
        store.wait()


def whole(memory=pltpu.VMEM):
    return pl.BlockSpec(memory_space=memory)


def call(kernel, outs, flops, moved, *args, far_args=(), far_outs=(), scratch=()):
    def space(i, array, far):
        return whole(pltpu.HBM if i in far else pltpu.SMEM if array.ndim == 1 else pltpu.VMEM)

    shapes = [jax.ShapeDtypeStruct(shape, dtype) for shape, dtype in outs]
    return pl.pallas_call(
        kernel,
        out_shape=shapes,
        in_specs=[space(i, arg, far_args) for i, arg in enumerate(args)],
        out_specs=[space(i, shape, far_outs) for i, shape in enumerate(shapes)],
        scratch_shapes=list(scratch),
        compiler_params=pltpu.CompilerParams(vmem_limit_bytes=VMEM),
        cost_estimate=pl.CostEstimate(flops=flops, bytes_accessed=moved, transcendentals=0),
    )(*args)


def local(tokens, segment_ids, w_query, w_key, w_value, grad_out):
    tok_rows = tokens[0]
    tok_count, depth = tok_rows.shape
    heads = w_query.shape[1]
    bf16 = jnp.bfloat16
    core = lax.axis_index("c")
    core_arg = core.reshape(1).astype(jnp.int32)
    flops, moved = 2 * tok_count * depth * 3 * heads, 3 * 2 * tok_count * depth

    weight_part = pltpu.VMEM((depth // 4, 3 * heads), bf16)
    tok_part = pltpu.VMEM((tok_count, depth // 4), bf16)

    start = (core * 64 + lax.axis_index("yl") * 32).reshape(1).astype(jnp.int32)
    (quarter,) = call(
        spread_kernel,
        [((8, 32, 3 * heads), bf16)],
        0,
        9 * 32 * 3 * heads * 2,
        start,
        *(pltpu.with_memory_space_constraint(w, pltpu.HBM) for w in (w_query, w_key, w_value)),
        far_args=(1, 2, 3),
        scratch=[pltpu.VMEM((3, 32, heads), bf16), pltpu.SemaphoreType.DMA((3,))],
    )
    far = lax.all_to_all(quarter, ("zh", "xlh"), 0, 0)
    half = cube_exchange(jnp.broadcast_to(far, (8,) + far.shape))
    other_half = lax.ppermute(half, "c", SWAP)
    full_weight, sent = call(
        project_kernel,
        [((depth, 3 * heads), bf16), ((tok_count, 4 * heads), bf16)],
        flops,
        moved,
        core_arg,
        tok_rows,
        half,
        other_half,
        grad_out[0],
        far_outs=(0,),
        scratch=[weight_part] * 4 + [pltpu.SemaphoreType.DMA((4,))],
    )

    device = lax.axis_index(FSDP)
    prior_ids, own_ids, next_ids = (
        lax.dynamic_slice_in_dim(segment_ids, jnp.clip(device + i, 0, 31) * tok_count, tok_count, axis=1)
        for i in (-1, 0, 1)
    )
    prior_ids = jnp.where(device > 0, prior_ids, -1)
    next_ids = jnp.where(device < 31, next_ids, -2)
    earlier = shifted(sent[:, heads : 3 * heads], 1)
    later = shifted(sent, -1)
    parts = (8, 8, 32, 3 * heads)
    attn, grad_proj, mine, other = call(
        attend_kernel,
        [
            ((tok_count, heads), bf16),
            ((tok_count, 3 * heads), bf16),
            (parts, bf16),
            (parts, bf16),
        ],
        flops + 14 * 4 * tok_count * tok_count * heads,
        moved,
        core_arg,
        pltpu.with_memory_space_constraint(tok_rows, pltpu.HBM),
        sent,
        earlier,
        later,
        prior_ids,
        own_ids,
        next_ids,
        far_args=(1,),
        scratch=[pltpu.VMEM((tok_count, depth), bf16), pltpu.SemaphoreType.DMA],
    )
    swapped = lax.ppermute(other, "c", SWAP)
    (grad_input,) = call(
        back_kernel,
        [((tok_count, depth), bf16)],
        flops,
        moved,
        grad_proj,
        full_weight,
        far_args=(1,),
        far_outs=(0,),
        scratch=[weight_part] * 4 + [tok_part] * 4 + [pltpu.SemaphoreType.DMA((4,))] * 2,
    )
    swapped, grad_input = lax.optimization_barrier((swapped, grad_input))
    chip = (mine.astype(jnp.float32) + swapped.astype(jnp.float32)).astype(jnp.bfloat16)
    cube = jnp.sum(cube_exchange(chip).astype(jnp.float32), axis=0)
    rows = cube.astype(jnp.bfloat16).reshape(64, 4, 3 * heads)
    rows = lax.all_to_all(rows, ("zh", "xlh", "yh", "xh"), 0, 0)
    count = math.prod(lax.axis_size(name) for name in FSDP + DP) * tok_count
    grads = jnp.sum(rows.astype(jnp.float32), axis=0) * (1.0 / math.sqrt(count))
    return (
        attn[None],
        grad_input[None],
        grads[:, :heads],
        grads[:, heads : 2 * heads],
        grads[:, 2 * heads :],
    )


def solution(mesh):
    fine = Mesh(mesh.devices.reshape(SIZES), FSDP + DP)
    rows = P(DP, FSDP, None)
    weight = P(FSDP, None)
    gradient = P(FSDP + DP, None)
    return jax.shard_map(
        local,
        mesh=fine,
        in_specs=(rows, P(DP, None), weight, weight, weight, rows),
        out_specs=(rows, rows, gradient, gradient, gradient),
        check_vma=False,
    )
```
